256 devices in a mesh: dp: 2 (over y_hi), expert: 128 (over x, y_lo, z, core).
Axes of the slice: x: 4, y: 4 (y_hi: 2, y_lo: 2; y = y_hi * 2 + y_lo), z: 8, core: 2. Of those that a mesh axis runs over, the one named last changes fastest.
Arguments:
- tokens: bfloat16 [512, 256, 1280], P(('dp', 'expert')), may hold values from -6 to 6
- norm_gain: float32 [1280], replicated, may hold values from 0.1 to 1.9
- slot_params: bfloat16 [1280, 128], replicated, may hold values from -0.15625 to 0.15625
- logit_scale: float32 [1], replicated, may hold values from 24 to 72
- expert_up: bfloat16 [128, 2560, 1280], P('expert', 'dp'), may hold values from -1.25 to 1.25
- expert_down: bfloat16 [128, 2560, 1280], P('expert', 'dp'), may hold values from -0.3125 to 0.3125
Outputs:
- mixed: bfloat16 [512, 256, 1280], P(('dp', 'expert'))
The draws below stay inside these ranges and needn't reach their ends.
All inputs are finite; a program needn't handle non-finite values.
Results may differ from the reference program's by a relative error of at most 0.019.
Values may be sent and summed in bfloat16 or wider, within the bound.
No kernel may reach another device: no remote copies, remote signals or barrier semaphores. Data moves between devices by JAX's collectives and lax.ppermute only.
A program may use at most 64 MiB of HBM per device.

```python
import math
import jax
import jax.numpy as jnp
from jax import lax

D = 1280
FF = 2560
TOK = 256
EXPERTS = 128
IMAGES = 512
N_DP = 2


def block_levels(rng, extent, shards, smallest, high):
    loudness, own = 1.0, jax.random.fold_in(rng, 6)
    for axis_at, parts in shards:
        draws = jnp.exp(jax.random.uniform(jax.random.fold_in(own, axis_at), (parts,), jnp.float32, smallest / len(shards), high / len(shards)))
        loudness = loudness * jnp.repeat(draws, extent[axis_at] // parts).reshape([-1 if axis == axis_at else 1 for axis in range(len(extent))])
    return loudness


def noise(stream_key, shape, width, limit, cuts=(), kind=jnp.bfloat16):
    drawn = jax.random.normal(stream_key, shape, jnp.float32) * width
    if len(cuts) > 0:
        drawn = block_levels(stream_key, shape, cuts, -0.22, 0.18) * drawn
    return jnp.clip(drawn, min=-limit, max=limit).astype(kind)


def setup_inputs(seed: int = 0) -> dict:
    key_of = jax.random.split(jax.random.key(seed), 7)
    return {
        "tokens": noise(key_of[0], (IMAGES, TOK, D), 1.0, 6.0, ((0, 256),)),
        "norm_gain": jnp.clip(1.0 + 0.18 * jax.random.normal(key_of[1], (D,), jnp.float32), 0.1, 1.9),
        "slot_params": noise(key_of[2], (D, EXPERTS), D ** -0.5, 0.15625),
        "logit_scale": jnp.clip(jnp.exp(jax.random.uniform(key_of[3], (1,), jnp.float32, math.log(24.0), math.log(72.0))), 24.0, 72.0),
        "expert_up": noise(key_of[4], (EXPERTS, FF, D), (D // 64) ** -0.5, 1.25, ((0, 128), (1, 2))),
        "expert_down": noise(key_of[5], (EXPERTS, FF, D), (FF // 8) ** -0.5, 0.3125, ((0, 128), (1, 2))),
    }


def normalize_tokens(values, norm_gain):
    floats = values.astype(jnp.float32)
    centred = floats - lax.optimization_barrier(jnp.mean(floats, axis=-1, keepdims=True))
    variance = lax.optimization_barrier(jnp.mean(centred * centred, axis=-1, keepdims=True))
    return (centred * lax.rsqrt(variance + 1e-06) * norm_gain).astype(jnp.bfloat16)

def image_slots(image, norm_gain, slot_params, logit_scale):
    normed = normalize_tokens(image, norm_gain)
    normed_f = normed.astype(jnp.float32)
    params_f = slot_params.astype(jnp.float32)
    scores = jnp.dot(normed_f, params_f)
    token_norm = jnp.sqrt(lax.optimization_barrier(jnp.sum(normed_f * normed_f, axis=-1)) + 1e-06)
    param_norm = jnp.sqrt(lax.optimization_barrier(jnp.sum(params_f * params_f, axis=0)) + 1e-06)
    logits = logit_scale[0] * scores / (token_norm[:, None] * param_norm[None, :])
    expo = jnp.exp(logits)
    dispatch = (expo / lax.optimization_barrier(jnp.sum(expo, axis=0, keepdims=True))).astype(jnp.bfloat16)
    combine = (expo / lax.optimization_barrier(jnp.sum(expo, axis=1, keepdims=True))).astype(jnp.bfloat16)
    slot_inputs = jnp.dot(dispatch.astype(jnp.float32).T, normed_f).astype(jnp.bfloat16)
    return (slot_inputs, combine)

def expert_apply(slot_rows, up_matrix, down_matrix):
    hidden = jax.nn.gelu(jnp.dot(slot_rows, up_matrix.T, preferred_element_type=jnp.float32), approximate=False).astype(jnp.bfloat16)
    groups = N_DP
    hidden_g = hidden.astype(jnp.float32).reshape(hidden.shape[0], groups, FF // groups)
    down_g = down_matrix.astype(jnp.float32).reshape(groups, FF // groups, D)
    pieces = jnp.einsum('rkf,kfd->krd', hidden_g, down_g).astype(jnp.bfloat16)
    return lax.optimization_barrier(jnp.sum(pieces.astype(jnp.float32), axis=0)).astype(jnp.bfloat16)

def reference(tokens, norm_gain, slot_params, logit_scale, expert_up, expert_down):
    slot_inputs, combine = lax.map(lambda image: image_slots(image, norm_gain, slot_params, logit_scale), tokens)
    by_expert = jnp.swapaxes(slot_inputs, 0, 1)
    slot_outputs = lax.map(lambda item: expert_apply(item[0], item[1], item[2]), (by_expert, expert_up, expert_down))
    by_image = jnp.swapaxes(slot_outputs, 0, 1)

    def mix_image(item):
        return jnp.dot(item[0], item[1], preferred_element_type=jnp.float32).astype(jnp.bfloat16)
    return lax.map(mix_image, (combine, by_image))
```

```python
import jax
import jax.numpy as jnp
from jax import lax
from jax.experimental import pallas as pl
from jax.experimental.pallas import tpu as pltpu
from jax.sharding import PartitionSpec as P

BF16 = jnp.bfloat16
F32 = jnp.float32
VMEM_LIMIT = 24 * 1024 * 1024


def halves(value):
    middle = value.shape[-1] // 2
    return value[:, :middle], value[:, middle:]


def route_kernel(tokens_ref, gain_ref, params_ref, scale_ref, slots_ref, combine_ref, normed_ref):
    tokens, width = normed_ref.shape
    gain = gain_ref[...]
    norms = []
    block = 64
    for at in range(0, tokens, block):
        rows = pl.ds(at, block)
        floats = tokens_ref[0, rows, :].astype(F32)
        centred = floats - jnp.mean(floats, axis=-1, keepdims=True)
        variance = jnp.mean(centred * centred, axis=-1, keepdims=True)
        normed = (centred * lax.rsqrt(variance + 1e-06) * gain).astype(BF16)
        normed_ref[rows, :] = normed
        normed_f = normed.astype(F32)
        norms.append(jnp.sum(normed_f * normed_f, axis=-1, keepdims=True))
    token_norm = jnp.sqrt(jnp.concatenate(norms, axis=0) + 1e-06)
    params = params_ref[...]
    params_f = params.astype(F32)
    param_norm = jnp.sqrt(jnp.sum(params_f * params_f, axis=0, keepdims=True) + 1e-06)
    normed = normed_ref[...]
    scores = jnp.dot(normed, params, preferred_element_type=F32)
    logits = scale_ref[0] * scores / (token_norm * param_norm)
    expo = jnp.exp(logits)
    dispatch = (expo / jnp.sum(expo, axis=0, keepdims=True)).astype(BF16)
    combine_ref[...] = (expo / jnp.sum(expo, axis=1, keepdims=True)).astype(BF16)
    slots = lax.dot_general(
        dispatch, normed, (((0,), (0,)), ((), ())), preferred_element_type=F32
    ).astype(BF16)
    slots_ref[:, 0, :], slots_ref[:, 1, :] = halves(slots)


def route(tokens, norm_gain, slot_params, logit_scale, image):
    _, count, width = tokens.shape
    slots = slot_params.shape[1]
    return pl.pallas_call(
        route_kernel,
        grid=(1,),
        in_specs=[
            pl.BlockSpec((1, count, width), lambda i: (image, 0, 0)),
            pl.BlockSpec((1, width), lambda i: (0, 0)),
            pl.BlockSpec((width, slots), lambda i: (0, 0)),
            pl.BlockSpec(memory_space=pltpu.SMEM),
        ],
        out_specs=[
            pl.BlockSpec((slots, 2, width // 2), lambda i: (0, 0, 0)),
            pl.BlockSpec((count, slots), lambda i: (0, 0)),
        ],
        out_shape=[
            jax.ShapeDtypeStruct((slots, 2, width // 2), BF16),
            jax.ShapeDtypeStruct((count, slots), BF16),
        ],
        scratch_shapes=[pltpu.VMEM((count, width), BF16)],
        compiler_params=pltpu.CompilerParams(vmem_limit_bytes=VMEM_LIMIT),
        cost_estimate=pl.CostEstimate(
            flops=4 * count * width * slots, bytes_accessed=2 * count * width * 2, transcendentals=count * slots
        ),
        name="route",
    )(tokens, norm_gain.reshape(1, width), slot_params, logit_scale)


def expert_kernel(rows_ref, up_ref, down_ref, out_ref):
    left, right = rows_ref[:, 0, :], rows_ref[:, 1, :]
    middle = left.shape[-1]
    hidden_units = up_ref.shape[1]
    block = 256
    total = None
    for at in range(0, hidden_units, block):
        units = pl.ds(at, block)
        over_features = (((1,), (1,)), ((), ()))
        before = lax.dot_general(
            left, up_ref[0, units, :middle], over_features, preferred_element_type=F32
        ) + lax.dot_general(right, up_ref[0, units, middle:], over_features, preferred_element_type=F32)
        hidden = (before * (0.5 + 0.5 * lax.erf(before * (0.5**0.5)))).astype(BF16)
        term = jnp.dot(hidden, down_ref[0, units, :], preferred_element_type=F32)
        total = term if total is None else total + term
    out_ref[:, 0, :], out_ref[:, 1, :] = halves(total.astype(BF16))


def expert(rows, up_matrix, down_matrix):
    count = rows.shape[0]
    _, hidden_units, width = up_matrix.shape
    vmem = pl.BlockSpec(memory_space=pltpu.VMEM)
    return pl.pallas_call(
        expert_kernel,
        in_specs=[vmem, vmem, vmem],
        out_specs=vmem,
        out_shape=jax.ShapeDtypeStruct(rows.shape, BF16),
        compiler_params=pltpu.CompilerParams(vmem_limit_bytes=VMEM_LIMIT),
        cost_estimate=pl.CostEstimate(
            flops=4 * count * width * hidden_units,
            bytes_accessed=4 * hidden_units * width,
            transcendentals=count * hidden_units,
        ),
        name="expert",
    )(rows, up_matrix, down_matrix)


def mix_kernel(combine_ref, slots_ref, *refs):
    out_ref = refs[-1]
    middle = slots_ref.shape[-1]
    combine = combine_ref[...]
    for half in range(2):
        out_ref[0, :, half * middle : (half + 1) * middle] = jnp.dot(
            combine, slots_ref[:, half, :], preferred_element_type=F32
        ).astype(BF16)


def mix(combine, slot_outputs, image, images, earlier):
    count, slots = combine.shape
    width = 2 * slot_outputs.shape[-1]
    operands = [combine, slot_outputs] + ([] if earlier is None else [earlier])
    in_specs = [
        pl.BlockSpec((count, slots), lambda i: (0, 0)),
        pl.BlockSpec(slot_outputs.shape, lambda i: (0, 0, 0)),
    ] + ([] if earlier is None else [pl.BlockSpec(memory_space=pl.ANY)])
    return pl.pallas_call(
        mix_kernel,
        grid=(1,),
        in_specs=in_specs,
        out_specs=pl.BlockSpec((1, count, width), lambda i: (image, 0, 0)),
        out_shape=jax.ShapeDtypeStruct((images, count, width), BF16),
        input_output_aliases={} if earlier is None else {2: 0},
        compiler_params=pltpu.CompilerParams(vmem_limit_bytes=VMEM_LIMIT),
        cost_estimate=pl.CostEstimate(
            flops=2 * count * width * slots, bytes_accessed=2 * count * width, transcendentals=0
        ),
        name="mix",
    )(*operands)


def swap_dp(value):
    return lax.ppermute(value, "dp", [(0, 1), (1, 0)])


def exchange(value):
    return lax.all_to_all(value, "expert", split_axis=0, concat_axis=0, tiled=True)


def local(tokens, norm_gain, slot_params, logit_scale, expert_up, expert_down):
    images = tokens.shape[0]
    combines, mixed = [], None
    returned = []
    for image in range(images):
        slot_inputs, combine = route(tokens, norm_gain, slot_params, logit_scale, image)
        combines.append(combine)
        arrived = exchange(slot_inputs)
        partner = swap_dp(arrived)
        kept = expert(arrived, expert_up, expert_down)
        received = swap_dp(expert(partner, expert_up, expert_down))
        slot_outputs = (kept.astype(F32) + received.astype(F32)).astype(BF16)
        returned.append(exchange(slot_outputs))
    for image in range(images):
        mixed = mix(combines[image], returned[image], image, images, mixed)
    return mixed


def solution(mesh):
    placed = (
        P(("dp", "expert"), None, None),
        P(),
        P(),
        P(),
        P("expert", "dp", None),
        P("expert", "dp", None),
    )
    return jax.shard_map(
        local,
        mesh=mesh,
        in_specs=placed,
        out_specs=P(("dp", "expert"), None, None),
        check_vma=False,
    )
```

```python
import jax
import jax.numpy as jnp
from jax import lax
from jax.experimental import pallas as pl
from jax.experimental.pallas import tpu as pltpu
from jax.sharding import Mesh
from jax.sharding import PartitionSpec as P

BF16 = jnp.bfloat16
F32 = jnp.float32
MIB = 1024 * 1024
AXES = ("dp", "x", "y_lo", "z", "core")
SIZES = (2, 4, 2, 8, 2)
INNER = 16
PLANE = ("x", "z", "core")
RING = ("dp", "y_lo")
RING_SIZE = 4
IMAGES = 2
VMEM = pl.BlockSpec(memory_space=pltpu.VMEM)
HBM = pl.BlockSpec(memory_space=pltpu.HBM)


def limit(mib):
    return pltpu.CompilerParams(vmem_limit_bytes=mib * MIB)


def column_slots(slots):
    column = lax.broadcasted_iota(jnp.int32, (1, IMAGES * slots), 1)
    slot = lax.broadcasted_iota(jnp.int32, (slots, IMAGES * slots), 0)
    group = (column >> 1) & 1
    place = column >> 2
    y_lo = (group + lax.axis_index("y_lo")) & 1
    wanted = (place >> 4) * (2 * INNER) + y_lo * INNER + (place & (INNER - 1))
    return (slot == wanted).astype(BF16)


def route_kernel(
    tokens_hbm, gain_hbm, params_hbm, scale_hbm, slots_ref, combine_ref,
    tokens_ref, gain_ref, params_ref, scale_ref, normed_ref, sems
):
    images, tokens, width = tokens_ref.shape
    copies = [
        pltpu.make_async_copy(params_hbm, params_ref, sems.at[0]),
        pltpu.make_async_copy(tokens_hbm.at[0], tokens_ref.at[0], sems.at[1]),
        pltpu.make_async_copy(gain_hbm, gain_ref, sems.at[2]),
        pltpu.make_async_copy(scale_hbm, scale_ref, sems.at[3]),
        pltpu.make_async_copy(tokens_hbm.at[1], tokens_ref.at[1], sems.at[4]),
    ]
    for copy in copies:
        copy.start()
    slots = params_ref.shape[1]
    columns = column_slots(slots)
    copies[0].wait()
    params = jnp.dot(params_ref[...], columns, preferred_element_type=F32)
    param_scale = lax.rsqrt(jnp.sum(params * params, axis=0, keepdims=True) + 1e-06)
    params = params.astype(BF16)
    copies[2].wait()
    copies[3].wait()
    gain = gain_ref[...].reshape(1, width)
    image_of = lax.broadcasted_iota(jnp.int32, (1, images * slots), 1) & 1
    dispatches = []
    block = 64
    for image in range(images):
        copies[1 if image == 0 else 4].wait()
        squares = []
        for at in range(0, tokens, block):
            floats = tokens_ref[image, at : at + block, :].astype(F32)
            centred = floats - jnp.mean(floats, axis=-1, keepdims=True)
            variance = jnp.mean(centred * centred, axis=-1, keepdims=True)
            normed = (centred * lax.rsqrt(variance + 1e-06) * gain).astype(BF16)
            normed_ref[image * tokens + at : image * tokens + at + block, :] = normed
            normed_f = normed.astype(F32)
            squares.append(jnp.sum(normed_f * normed_f, axis=-1, keepdims=True))
        token_scale = scale_ref[0] * lax.rsqrt(jnp.concatenate(squares, axis=0) + 1e-06)
        normed = normed_ref[image * tokens : (image + 1) * tokens, :]
        scores = jnp.dot(normed, params, preferred_element_type=F32)
        expo = jnp.exp(scores * token_scale * param_scale)
        expo = jnp.where(image_of == image, expo, 0.0)
        over_tokens = jnp.sum(expo, axis=0, keepdims=True)
        over_tokens = jnp.where(image_of == image, over_tokens, 1.0)
        dispatches.append((expo * (1.0 / over_tokens)).astype(BF16))
        combine_ref[image, :, :] = (expo * (1.0 / jnp.sum(expo, axis=1, keepdims=True))).astype(BF16)
    gathered = lax.dot_general(
        jnp.concatenate(dispatches, axis=0),
        normed_ref[...],
        (((0,), (0,)), ((), ())),
        preferred_element_type=F32,
    ).astype(BF16)
    slots_ref[...] = gathered.reshape(slots_ref.shape)


def route(tokens, norm_gain, slot_params, logit_scale):
    images, count, width = tokens.shape
    slots = slot_params.shape[1]
    return pl.pallas_call(
        route_kernel,
        in_specs=[HBM] * 4,
        out_specs=[VMEM] * 2,
        out_shape=[
            jax.ShapeDtypeStruct((slots // 2, 2, images, width), BF16),
            jax.ShapeDtypeStruct((images, count, images * slots), BF16),
        ],
        scratch_shapes=[
            pltpu.VMEM(tokens.shape, BF16),
            pltpu.VMEM(norm_gain.shape, F32),
            pltpu.VMEM(slot_params.shape, BF16),
            pltpu.SMEM(logit_scale.shape, F32),
            pltpu.VMEM((images * count, width), BF16),
            pltpu.SemaphoreType.DMA((5,)),
        ],
        compiler_params=limit(60),
        name="route",
    )(tokens, norm_gain, slot_params, logit_scale)


def expert_parts(rows, up_matrix, down_matrix):
    before = lax.dot_general(rows, up_matrix, (((1,), (1,)), ((), ())), preferred_element_type=F32)
    hidden = (before * (0.5 + 0.5 * lax.erf(before * (0.5**0.5)))).astype(BF16)
    return jnp.dot(hidden, down_matrix, preferred_element_type=F32).astype(BF16)


def first_expert_kernel(rows_ref, up_hbm, down_hbm, out_ref, up_ref, down_ref, sems):
    width = up_ref.shape[1]
    up_copy = pltpu.make_async_copy(up_hbm.at[0], up_ref, sems.at[0])
    down_copy = pltpu.make_async_copy(down_hbm.at[0], down_ref, sems.at[1])
    up_copy.start()
    down_copy.start()
    up_copy.wait()
    down_copy.wait()
    part = expert_parts(rows_ref[...].reshape(-1, width), up_ref[...], down_ref[...])
    out_ref[...] = part.reshape(out_ref.shape)


def first_expert(group, up_matrix, down_matrix):
    return pl.pallas_call(
        first_expert_kernel,
        in_specs=[VMEM, HBM, HBM],
        out_specs=[VMEM] * 3,
        out_shape=[
            jax.ShapeDtypeStruct(group.shape, BF16),
            jax.ShapeDtypeStruct(up_matrix.shape[1:], BF16),
            jax.ShapeDtypeStruct(down_matrix.shape[1:], BF16),
        ],
        scratch_shapes=[pltpu.SemaphoreType.DMA((2,))],
        compiler_params=limit(16),
        name="first_expert",
    )(group, up_matrix, down_matrix)


def expert_kernel(groups, *refs):
    up_ref, down_ref = refs[groups : groups + 2]
    outs = refs[groups + 2 :]
    width = up_ref.shape[1]
    flat = [ref[...].reshape(-1, width) for ref in refs[:groups]]
    count = flat[0].shape[0]
    rows = flat[0] if groups == 1 else jnp.concatenate(flat, axis=0)
    part = expert_parts(rows, up_ref[...], down_ref[...])
    for at, out_ref in enumerate(outs):
        out_ref[...] = part[at * count : (at + 1) * count].reshape(out_ref.shape)


def expert(groups, up_matrix, down_matrix):
    return pl.pallas_call(
        lambda *refs: expert_kernel(len(groups), *refs),
        in_specs=[VMEM] * (len(groups) + 2),
        out_specs=[VMEM] * len(groups),
        out_shape=[jax.ShapeDtypeStruct(group.shape, BF16) for group in groups],
        compiler_params=limit(16),
        name="expert",
    )(*groups, up_matrix, down_matrix)


def add_kernel(own_a_ref, own_b_ref, other_a_ref, other_b_ref, out_ref):
    for group, (a_ref, b_ref) in enumerate([(own_a_ref, own_b_ref), (other_a_ref, other_b_ref)]):
        out_ref[:, group, :, :] = (a_ref[...].astype(F32) + b_ref[...].astype(F32)).astype(BF16)


def add_parts(own, other):
    places, images, width = own[0].shape
    return pl.pallas_call(
        add_kernel,
        in_specs=[VMEM] * 4,
        out_specs=VMEM,
        out_shape=jax.ShapeDtypeStruct((places, 2, images, width), BF16),
        compiler_params=limit(16),
        name="add_parts",
    )(*own, *other)


def mix_kernel(combine_ref, slots_ref, out_hbm, out_ref, sems):
    images, _, columns = combine_ref.shape
    slots = slots_ref[...].reshape(columns, -1)
    copies = []
    for image in range(images):
        out_ref[image, :, :] = jnp.dot(combine_ref[image], slots, preferred_element_type=F32).astype(BF16)
        copies.append(pltpu.make_async_copy(out_ref.at[image], out_hbm.at[image], sems.at[image]))
        copies[-1].start()
    for copy in copies:
        copy.wait()


def mix(combine, slot_outputs):
    images, count, _ = combine.shape
    mixed = jax.ShapeDtypeStruct((images, count, slot_outputs.shape[-1]), BF16)
    return pl.pallas_call(
        mix_kernel,
        in_specs=[VMEM] * 2,
        out_specs=HBM,
        out_shape=mixed,
        scratch_shapes=[pltpu.VMEM(mixed.shape, BF16), pltpu.SemaphoreType.DMA((images,))],
        compiler_params=limit(16),
        name="mix",
    )(combine, slot_outputs)


def around(value, step):
    return lax.ppermute(value, RING, [(at, (at + step) % RING_SIZE) for at in range(RING_SIZE)])


def exchange(value):
    return lax.all_to_all(value, PLANE, split_axis=0, concat_axis=0, tiled=True)


def local(tokens, norm_gain, slot_params, logit_scale, expert_up, expert_down):
    slot_inputs, combine = route(tokens, norm_gain, slot_params, logit_scale)
    arrived = exchange(slot_inputs)
    own, other = arrived[:, 0], arrived[:, 1]
    below, above = around(other, 1), around(other, -1)
    kept, up_matrix, down_matrix = first_expert(own, expert_up, expert_down)
    own, kept = lax.optimization_barrier((own, kept))
    across = around(own, 2)
    below, above = expert([below, above], up_matrix, down_matrix)
    from_above, from_below = around(below, -1), around(above, 1)
    (across,) = expert([across], up_matrix, down_matrix)
    slot_outputs = add_parts((kept, around(across, 2)), (from_above, from_below))
    return mix(combine, exchange(slot_outputs))


def solution(mesh):
    fine = Mesh(mesh.devices.reshape(SIZES), AXES)
    expert_axes = AXES[1:]
    placed = (
        P(AXES, None, None),
        P(),
        P(),
        P(),
        P(expert_axes, "dp", None),
        P(expert_axes, "dp", None),
    )
    return jax.shard_map(
        local,
        mesh=fine,
        in_specs=placed,
        out_specs=P(AXES, None, None),
        check_vma=False,
    )
```

```python
import jax
import jax.numpy as jnp
from jax import lax
from jax.experimental import pallas as pl
from jax.experimental.pallas import tpu as pltpu
from jax.sharding import Mesh
from jax.sharding import PartitionSpec as P

BF16 = jnp.bfloat16
F32 = jnp.float32
MIB = 1024 * 1024
AXES = ("dp", "x", "y_lo", "z", "core")
SIZES = (2, 4, 2, 8, 2)
INNER = 16
PLANE = ("x", "z", "core")
RING = ("dp", "y_lo")
EVEN, ODD, ACROSS = ((0, 1), (2, 3)), ((1, 2), (3, 0)), ((0, 2), (1, 3))
IMAGES = 2
VMEM = pl.BlockSpec(memory_space=pltpu.VMEM)
HBM = pl.BlockSpec(memory_space=pltpu.HBM)


def limit(mib):
    return pltpu.CompilerParams(vmem_limit_bytes=mib * MIB)


def column_slots(slots):
    column = lax.broadcasted_iota(jnp.int32, (1, IMAGES * slots), 1)
    slot = lax.broadcasted_iota(jnp.int32, (slots, IMAGES * slots), 0)
    group = (column >> 1) & 1
    place = column >> 2
    y_lo = (group + lax.axis_index("y_lo")) & 1
    wanted = (place >> 4) * (2 * INNER) + y_lo * INNER + (place & (INNER - 1))
    return (slot == wanted).astype(BF16)


def route_kernel(
    tokens_hbm, gain_hbm, params_hbm, scale_hbm, slots_ref, combine_ref,
    tokens_ref, gain_ref, params_ref, scale_ref, normed_ref, sems
):
    images, tokens, width = tokens_ref.shape
    copies = [
        pltpu.make_async_copy(params_hbm, params_ref, sems.at[0]),
        pltpu.make_async_copy(tokens_hbm.at[0], tokens_ref.at[0], sems.at[1]),
        pltpu.make_async_copy(gain_hbm, gain_ref, sems.at[2]),
        pltpu.make_async_copy(scale_hbm, scale_ref, sems.at[3]),
        pltpu.make_async_copy(tokens_hbm.at[1], tokens_ref.at[1], sems.at[4]),
    ]
    for copy in copies:
        copy.start()
    slots = params_ref.shape[1]
    columns = column_slots(slots)
    copies[0].wait()
    params = jnp.dot(params_ref[...], columns, preferred_element_type=F32)
    param_scale = lax.rsqrt(jnp.sum(params * params, axis=0, keepdims=True) + 1e-06)
    params = params.astype(BF16)
    copies[2].wait()
    copies[3].wait()
    gain = gain_ref[...].reshape(1, width)
    image_of = lax.broadcasted_iota(jnp.int32, (1, images * slots), 1) & 1
    dispatches = []
    block = 64
    for image in range(images):
        copies[1 if image == 0 else 4].wait()
        squares = []
        for at in range(0, tokens, block):
            floats = tokens_ref[image, at : at + block, :].astype(F32)
            centred = floats - jnp.mean(floats, axis=-1, keepdims=True)
            variance = jnp.mean(centred * centred, axis=-1, keepdims=True)
            normed = (centred * lax.rsqrt(variance + 1e-06) * gain).astype(BF16)
            normed_ref[image * tokens + at : image * tokens + at + block, :] = normed
            normed_f = normed.astype(F32)
            squares.append(jnp.sum(normed_f * normed_f, axis=-1, keepdims=True))
        token_scale = scale_ref[0] * lax.rsqrt(jnp.concatenate(squares, axis=0) + 1e-06)
        normed = normed_ref[image * tokens : (image + 1) * tokens, :]
        scores = jnp.dot(normed, params, preferred_element_type=F32)
        expo = jnp.exp(scores * token_scale * param_scale)
        expo = jnp.where(image_of == image, expo, 0.0)
        over_tokens = jnp.sum(expo, axis=0, keepdims=True)
        over_tokens = jnp.where(image_of == image, over_tokens, 1.0)
        dispatches.append((expo * (1.0 / over_tokens)).astype(BF16))
        combine_ref[image, :, :] = (expo * (1.0 / jnp.sum(expo, axis=1, keepdims=True))).astype(BF16)
    gathered = lax.dot_general(
        jnp.concatenate(dispatches, axis=0),
        normed_ref[...],
        (((0,), (0,)), ((), ())),
        preferred_element_type=F32,
    ).astype(BF16)
    slots_ref[...] = gathered.reshape(slots_ref.shape)


def route(tokens, norm_gain, slot_params, logit_scale):
    images, count, width = tokens.shape
    slots = slot_params.shape[1]
    return pl.pallas_call(
        route_kernel,
        in_specs=[HBM] * 4,
        out_specs=[VMEM] * 2,
        out_shape=[
            jax.ShapeDtypeStruct((slots // 2, 2, images, width), BF16),
            jax.ShapeDtypeStruct((images, count, images * slots), BF16),
        ],
        scratch_shapes=[
            pltpu.VMEM(tokens.shape, BF16),
            pltpu.VMEM(norm_gain.shape, F32),
            pltpu.VMEM(slot_params.shape, BF16),
            pltpu.SMEM(logit_scale.shape, F32),
            pltpu.VMEM((images * count, width), BF16),
            pltpu.SemaphoreType.DMA((5,)),
        ],
        compiler_params=limit(60),
        name="route",
    )(tokens, norm_gain, slot_params, logit_scale)


def expert_parts(rows, up_matrix, down_matrix):
    before = lax.dot_general(rows, up_matrix, (((1,), (1,)), ((), ())), preferred_element_type=F32)
    hidden = (before * (0.5 + 0.5 * lax.erf(before * (0.5**0.5)))).astype(BF16)
    return jnp.dot(hidden, down_matrix, preferred_element_type=F32).astype(BF16)


def first_expert_kernel(rows_ref, up_hbm, down_hbm, out_ref, up_ref, down_ref, sems):
    width = up_ref.shape[1]
    up_copy = pltpu.make_async_copy(up_hbm.at[0], up_ref, sems.at[0])
    down_copy = pltpu.make_async_copy(down_hbm.at[0], down_ref, sems.at[1])
    up_copy.start()
    down_copy.start()
    up_copy.wait()
    down_copy.wait()
    part = expert_parts(rows_ref[...].reshape(-1, width), up_ref[...], down_ref[...])
    out_ref[...] = part.reshape(out_ref.shape)


def first_expert(group, up_matrix, down_matrix):
    return pl.pallas_call(
        first_expert_kernel,
        in_specs=[VMEM, HBM, HBM],
        out_specs=[VMEM] * 3,
        out_shape=[
            jax.ShapeDtypeStruct(group.shape, BF16),
            jax.ShapeDtypeStruct(up_matrix.shape[1:], BF16),
            jax.ShapeDtypeStruct(down_matrix.shape[1:], BF16),
        ],
        scratch_shapes=[pltpu.SemaphoreType.DMA((2,))],
        compiler_params=limit(16),
        name="first_expert",
    )(group, up_matrix, down_matrix)


def expert_kernel(groups, *refs):
    up_ref, down_ref = refs[groups : groups + 2]
    outs = refs[groups + 2 :]
    width = up_ref.shape[1]
    flat = [ref[...].reshape(-1, width) for ref in refs[:groups]]
    count = flat[0].shape[0]
    rows = flat[0] if groups == 1 else jnp.concatenate(flat, axis=0)
    part = expert_parts(rows, up_ref[...], down_ref[...])
    for at, out_ref in enumerate(outs):
        out_ref[...] = part[at * count : (at + 1) * count].reshape(out_ref.shape)


def expert(groups, up_matrix, down_matrix):
    return pl.pallas_call(
        lambda *refs: expert_kernel(len(groups), *refs),
        in_specs=[VMEM] * (len(groups) + 2),
        out_specs=[VMEM] * len(groups),
        out_shape=[jax.ShapeDtypeStruct(group.shape, BF16) for group in groups],
        compiler_params=limit(16),
        name="expert",
    )(*groups, up_matrix, down_matrix)


def add_kernel(own_a_ref, own_b_ref, other_a_ref, other_b_ref, out_ref):
    for group, (a_ref, b_ref) in enumerate([(own_a_ref, own_b_ref), (other_a_ref, other_b_ref)]):
        out_ref[:, group, :, :] = (a_ref[...].astype(F32) + b_ref[...].astype(F32)).astype(BF16)


def add_parts(own, other):
    places, images, width = own[0].shape
    return pl.pallas_call(
        add_kernel,
        in_specs=[VMEM] * 4,
        out_specs=VMEM,
        out_shape=jax.ShapeDtypeStruct((places, 2, images, width), BF16),
        compiler_params=limit(16),
        name="add_parts",
    )(*own, *other)


def mix_kernel(combine_ref, slots_ref, out_hbm, out_ref, sems):
    images, _, columns = combine_ref.shape
    slots = slots_ref[...].reshape(columns, -1)
    copies = []
    for image in range(images):
        out_ref[image, :, :] = jnp.dot(combine_ref[image], slots, preferred_element_type=F32).astype(BF16)
        copies.append(pltpu.make_async_copy(out_ref.at[image], out_hbm.at[image], sems.at[image]))
        copies[-1].start()
    for copy in copies:
        copy.wait()


def mix(combine, slot_outputs):
    images, count, _ = combine.shape
    mixed = jax.ShapeDtypeStruct((images, count, slot_outputs.shape[-1]), BF16)
    return pl.pallas_call(
        mix_kernel,
        in_specs=[VMEM] * 2,
        out_specs=HBM,
        out_shape=mixed,
        scratch_shapes=[pltpu.VMEM(mixed.shape, BF16), pltpu.SemaphoreType.DMA((images,))],
        compiler_params=limit(16),
        name="mix",
    )(combine, slot_outputs)


def pairwise(value, pairs):
    return lax.ppermute(value, RING, [(a, b) for a, b in pairs] + [(b, a) for a, b in pairs])


def exchange(value):
    return lax.all_to_all(value, PLANE, split_axis=0, concat_axis=0, tiled=True)


def local(tokens, norm_gain, slot_params, logit_scale, expert_up, expert_down):
    slot_inputs, combine = route(tokens, norm_gain, slot_params, logit_scale)
    arrived = exchange(slot_inputs)
    own, other = arrived[:, 0], arrived[:, 1]
    odd, even = pairwise(other, ODD), pairwise(other, EVEN)
    across = pairwise(own, ACROSS)
    kept, up_matrix, down_matrix = first_expert(own, expert_up, expert_down)
    even, odd = expert([even, odd], up_matrix, down_matrix)
    odd, even = pairwise(odd, ODD), pairwise(even, EVEN)
    (across,) = expert([across], up_matrix, down_matrix)
    slot_outputs = add_parts((kept, pairwise(across, ACROSS)), (even, odd))
    return mix(combine, exchange(slot_outputs))


def solution(mesh):
    fine = Mesh(mesh.devices.reshape(SIZES), AXES)
    expert_axes = AXES[1:]
    placed = (
        P(AXES, None, None),
        P(),
        P(),
        P(),
        P(expert_axes, "dp", None),
        P(expert_axes, "dp", None),
    )
    return jax.shard_map(
        local,
        mesh=fine,
        in_specs=placed,
        out_specs=P(AXES, None, None),
        check_vma=False,
    )
```

```python
import jax
import jax.numpy as jnp
from jax import lax
from jax.experimental import pallas as pl
from jax.experimental.pallas import tpu as pltpu
from jax.sharding import Mesh
from jax.sharding import PartitionSpec as P

BF16 = jnp.bfloat16
F32 = jnp.float32
MIB = 1024 * 1024
AXES = ("dp", "x", "y_lo", "z", "core")
SIZES = (2, 4, 2, 8, 2)
INNER = 16
PLANE = ("x", "z", "core")
RING = ("dp", "y_lo")
EVEN, ODD, ACROSS = ((0, 1), (2, 3)), ((1, 2), (3, 0)), ((0, 2), (1, 3))
IMAGES = 2
VMEM = pl.BlockSpec(memory_space=pltpu.VMEM)
HBM = pl.BlockSpec(memory_space=pltpu.HBM)


def limit(mib):
    return pltpu.CompilerParams(vmem_limit_bytes=mib * MIB)


def column_slots(slots):
    column = lax.broadcasted_iota(jnp.int32, (1, IMAGES * slots), 1)
    slot = lax.broadcasted_iota(jnp.int32, (slots, IMAGES * slots), 0)
    group = (column >> 1) & 1
    place = column >> 2
    y_lo = (group + lax.axis_index("y_lo")) & 1
    wanted = (place >> 4) * (2 * INNER) + y_lo * INNER + (place & (INNER - 1))
    return (slot == wanted).astype(BF16)


def route_kernel(
    tokens_hbm, gain_hbm, params_hbm, scale_hbm, slots_hbm, combine_hbm,
    tokens_ref, gain_ref, params_ref, scale_ref, normed_ref, slots_ref, combine_ref, sems
):
    images, tokens, width = tokens_ref.shape
    copies = [
        pltpu.make_async_copy(params_hbm, params_ref, sems.at[0]),
        pltpu.make_async_copy(tokens_hbm.at[0], tokens_ref.at[0], sems.at[1]),
        pltpu.make_async_copy(gain_hbm, gain_ref, sems.at[2]),
        pltpu.make_async_copy(scale_hbm, scale_ref, sems.at[3]),
        pltpu.make_async_copy(tokens_hbm.at[1], tokens_ref.at[1], sems.at[4]),
    ]
    for copy in copies:
        copy.start()
    slots = params_ref.shape[1]
    columns = column_slots(slots)
    copies[0].wait()
    params = jnp.dot(params_ref[...], columns, preferred_element_type=F32)
    param_scale = lax.rsqrt(jnp.sum(params * params, axis=0, keepdims=True) + 1e-06)
    params = params.astype(BF16)
    copies[2].wait()
    copies[3].wait()
    gain = gain_ref[...].reshape(1, width)
    image_of = lax.broadcasted_iota(jnp.int32, (1, images * slots), 1) & 1
    dispatches = []
    block = 64
    for image in range(images):
        copies[1 if image == 0 else 4].wait()
        squares = []
        for at in range(0, tokens, block):
            floats = tokens_ref[image, at : at + block, :].astype(F32)
            centred = floats - jnp.mean(floats, axis=-1, keepdims=True)
            variance = jnp.mean(centred * centred, axis=-1, keepdims=True)
            normed = (centred * lax.rsqrt(variance + 1e-06) * gain).astype(BF16)
            normed_ref[image * tokens + at : image * tokens + at + block, :] = normed
            normed_f = normed.astype(F32)
            squares.append(jnp.sum(normed_f * normed_f, axis=-1, keepdims=True))
        token_scale = scale_ref[0] * lax.rsqrt(jnp.concatenate(squares, axis=0) + 1e-06)
        normed = normed_ref[image * tokens : (image + 1) * tokens, :]
        scores = jnp.dot(normed, params, preferred_element_type=F32)
        expo = jnp.exp(scores * token_scale * param_scale)
        expo = jnp.where(image_of == image, expo, 0.0)
        over_tokens = jnp.sum(expo, axis=0, keepdims=True)
        over_tokens = jnp.where(image_of == image, over_tokens, 1.0)
        dispatches.append((expo * (1.0 / over_tokens)).astype(BF16))
        combine_ref[image, :, :] = (expo * (1.0 / jnp.sum(expo, axis=1, keepdims=True))).astype(BF16)
        copies.append(pltpu.make_async_copy(combine_ref.at[image], combine_hbm.at[image], sems.at[5 + image]))
        copies[-1].start()
    dispatch = jnp.concatenate(dispatches, axis=0)
    places = slots_ref.shape[0] // 2
    for half in range(2):
        part = slice(half * places, (half + 1) * places)
        gathered = lax.dot_general(
            dispatch[:, half * slots : (half + 1) * slots],
            normed_ref[...],
            (((0,), (0,)), ((), ())),
            preferred_element_type=F32,
        ).astype(BF16)
        slots_ref[part] = gathered.reshape(places, *slots_ref.shape[1:])
        copies.append(pltpu.make_async_copy(slots_ref.at[part], slots_hbm.at[part], sems.at[7 + half]))
        copies[-1].start()
    for copy in copies[5:]:
        copy.wait()


def route(tokens, norm_gain, slot_params, logit_scale):
    images, count, width = tokens.shape
    slots = slot_params.shape[1]
    return pl.pallas_call(
        route_kernel,
        in_specs=[HBM] * 4,
        out_specs=[HBM] * 2,
        out_shape=[
            jax.ShapeDtypeStruct((slots // 2, 2, images, width), BF16),
            jax.ShapeDtypeStruct((images, count, images * slots), BF16),
        ],
        scratch_shapes=[
            pltpu.VMEM(tokens.shape, BF16),
            pltpu.VMEM(norm_gain.shape, F32),
            pltpu.VMEM(slot_params.shape, BF16),
            pltpu.SMEM(logit_scale.shape, F32),
            pltpu.VMEM((images * count, width), BF16),
            pltpu.VMEM((slots // 2, 2, images, width), BF16),
            pltpu.VMEM((images, count, images * slots), BF16),
            pltpu.SemaphoreType.DMA((9,)),
        ],
        compiler_params=limit(60),
        name="route",
    )(tokens, norm_gain, slot_params, logit_scale)


def expert_parts(rows, up_matrix, down_matrix):
    before = jnp.dot(rows, up_matrix, preferred_element_type=F32)
    hidden = (before * (0.5 + 0.5 * lax.erf(before * (0.5**0.5)))).astype(BF16)
    return jnp.dot(hidden, down_matrix, preferred_element_type=F32).astype(BF16)


def first_expert_kernel(rows_ref, up_hbm, down_hbm, out_ref, up_ref, down_ref, sems):
    up_copy = pltpu.make_async_copy(up_hbm.at[0], up_ref, sems.at[0])
    down_copy = pltpu.make_async_copy(down_hbm.at[0], down_ref, sems.at[1])
    up_copy.start()
    down_copy.start()
    up_copy.wait()
    down_copy.wait()
    up_ref[...] = up_ref[...].T
    part = expert_parts(rows_ref[...], up_ref[...], down_ref[...])
    out_ref[...] = part


def first_expert(group, up_matrix, down_matrix):
    return pl.pallas_call(
        first_expert_kernel,
        in_specs=[VMEM, HBM, HBM],
        out_specs=[VMEM] * 3,
        out_shape=[
            jax.ShapeDtypeStruct(group.shape, BF16),
            jax.ShapeDtypeStruct(up_matrix.shape[:0:-1], BF16),
            jax.ShapeDtypeStruct(down_matrix.shape[1:], BF16),
        ],
        scratch_shapes=[pltpu.SemaphoreType.DMA((2,))],
        compiler_params=limit(16),
        name="first_expert",
    )(group, up_matrix, down_matrix)


def expert_kernel(groups, *refs):
    up_ref, down_ref = refs[groups : groups + 2]
    outs = refs[groups + 2 :]
    flat = [ref[...] for ref in refs[:groups]]
    count = flat[0].shape[0]
    rows = flat[0] if groups == 1 else jnp.concatenate(flat, axis=0)
    part = expert_parts(rows, up_ref[...], down_ref[...])
    for at, out_ref in enumerate(outs):
        out_ref[...] = part[at * count : (at + 1) * count]


def expert(groups, up_matrix, down_matrix):
    return pl.pallas_call(
        lambda *refs: expert_kernel(len(groups), *refs),
        in_specs=[VMEM] * (len(groups) + 2),
        out_specs=[VMEM] * len(groups),
        out_shape=[jax.ShapeDtypeStruct(group.shape, BF16) for group in groups],
        compiler_params=limit(16),
        name="expert",
    )(*groups, up_matrix, down_matrix)


def split_kernel(arrived_ref, own_ref, other_ref):
    own_ref[...] = arrived_ref[:, 0, :, :].reshape(own_ref.shape)
    other_ref[...] = arrived_ref[:, 1, :, :].reshape(other_ref.shape)


def split(arrived):
    places, _, images, width = arrived.shape
    group = jax.ShapeDtypeStruct((places * images, width), BF16)
    return pl.pallas_call(
        split_kernel,
        in_specs=[VMEM],
        out_specs=[VMEM] * 2,
        out_shape=[group, group],
        compiler_params=limit(16),
        name="split",
    )(arrived)


def add_kernel(own_a_ref, own_b_ref, other_a_ref, other_b_ref, out_ref):
    places, _, images, width = out_ref.shape
    for group, (a_ref, b_ref) in enumerate([(own_a_ref, own_b_ref), (other_a_ref, other_b_ref)]):
        total = (a_ref[...].astype(F32) + b_ref[...].astype(F32)).astype(BF16)
        out_ref[:, group, :, :] = total.reshape(places, images, width)


def add_parts(own, other):
    rows, width = own[0].shape
    return pl.pallas_call(
        add_kernel,
        in_specs=[VMEM] * 4,
        out_specs=VMEM,
        out_shape=jax.ShapeDtypeStruct((rows // IMAGES, 2, IMAGES, width), BF16),
        compiler_params=limit(16),
        name="add_parts",
    )(*own, *other)


def mix_kernel(combine_ref, slots_ref, out_hbm, out_ref, sems):
    images, _, columns = combine_ref.shape
    slots = slots_ref[...].reshape(columns, -1)
    copies = []
    half = combine_ref.shape[1] // 2
    for image in range(images):
        for at in range(2):
            part = slice(at * half, (at + 1) * half)
            mixed = jnp.dot(combine_ref[image, part, :], slots, preferred_element_type=F32)
            out_ref[image, part, :] = mixed.astype(BF16)
            copies.append(
                pltpu.make_async_copy(out_ref.at[image, part], out_hbm.at[image, part], sems.at[image, at])
            )
            copies[-1].start()
    for copy in copies:
        copy.wait()


def mix(combine, slot_outputs):
    images, count, _ = combine.shape
    mixed = jax.ShapeDtypeStruct((images, count, slot_outputs.shape[-1]), BF16)
    return pl.pallas_call(
        mix_kernel,
        in_specs=[VMEM] * 2,
        out_specs=HBM,
        out_shape=mixed,
        scratch_shapes=[pltpu.VMEM(mixed.shape, BF16), pltpu.SemaphoreType.DMA((images, 2))],
        compiler_params=limit(16),
        name="mix",
    )(combine, slot_outputs)


def pairwise(value, pairs):
    return lax.ppermute(value, RING, [(a, b) for a, b in pairs] + [(b, a) for a, b in pairs])


def exchange(value):
    return lax.all_to_all(value, PLANE, split_axis=0, concat_axis=0, tiled=True)


def local(tokens, norm_gain, slot_params, logit_scale, expert_up, expert_down):
    slot_inputs, combine = route(tokens, norm_gain, slot_params, logit_scale)
    arrived = exchange(slot_inputs)
    own, other = split(arrived)
    odd, even = pairwise(other, ODD), pairwise(other, EVEN)
    across = pairwise(own, ACROSS)
    kept, up_matrix, down_matrix = first_expert(own, expert_up, expert_down)
    even, odd = expert([even, odd], up_matrix, down_matrix)
    odd, even = pairwise(odd, ODD), pairwise(even, EVEN)
    (across,) = expert([across], up_matrix, down_matrix)
    slot_outputs = add_parts((kept, pairwise(across, ACROSS)), (even, odd))
    return mix(combine, exchange(slot_outputs))


def solution(mesh):
    fine = Mesh(mesh.devices.reshape(SIZES), AXES)
    expert_axes = AXES[1:]
    placed = (
        P(AXES, None, None),
        P(),
        P(),
        P(),
        P(expert_axes, "dp", None),
        P(expert_axes, "dp", None),
    )
    return jax.shard_map(
        local,
        mesh=fine,
        in_specs=placed,
        out_specs=P(AXES, None, None),
        check_vma=False,
    )
```

```python
import jax
import jax.numpy as jnp
from jax import lax
from jax.experimental import pallas as pl
from jax.experimental.pallas import tpu as pltpu
from jax.sharding import Mesh
from jax.sharding import PartitionSpec as P

BF16 = jnp.bfloat16
F32 = jnp.float32
MIB = 1024 * 1024
AXES = ("dp", "x", "y_lo", "z", "core")
SIZES = (2, 4, 2, 8, 2)
INNER = 16
PLANE = ("x", "z", "core")
RING = ("dp", "y_lo")
FIRST, SECOND, ACROSS = ((3, 2, 1, 0), (1, 0, 3, 2)), ((1, 0, 3, 2), (3, 2, 1, 0)), ((2, 3, 0, 1), (2, 3, 0, 1))
IMAGES = 2
VMEM = pl.BlockSpec(memory_space=pltpu.VMEM)
HBM = pl.BlockSpec(memory_space=pltpu.HBM)


def limit(mib):
    return pltpu.CompilerParams(vmem_limit_bytes=mib * MIB)


def column_slots(slots):
    column = lax.broadcasted_iota(jnp.int32, (1, IMAGES * slots), 1)
    slot = lax.broadcasted_iota(jnp.int32, (slots, IMAGES * slots), 0)
    group = (column >> 1) & 1
    place = column >> 2
    y_lo = (group + lax.axis_index("y_lo")) & 1
    wanted = (place >> 4) * (2 * INNER) + y_lo * INNER + (place & (INNER - 1))
    return (slot == wanted).astype(BF16)


def route_kernel(
    tokens_hbm, gain_hbm, params_hbm, scale_hbm, slots_hbm, combine_hbm,
    tokens_ref, gain_ref, params_ref, scale_ref, normed_ref, slots_ref, combine_ref, sems
):
    images, tokens, width = tokens_ref.shape
    copies = [
        pltpu.make_async_copy(params_hbm, params_ref, sems.at[0]),
        pltpu.make_async_copy(tokens_hbm.at[0], tokens_ref.at[0], sems.at[1]),
        pltpu.make_async_copy(gain_hbm, gain_ref, sems.at[2]),
        pltpu.make_async_copy(scale_hbm, scale_ref, sems.at[3]),
        pltpu.make_async_copy(tokens_hbm.at[1], tokens_ref.at[1], sems.at[4]),
    ]
    for copy in copies:
        copy.start()
    slots = params_ref.shape[1]
    columns = column_slots(slots)
    copies[0].wait()
    params = jnp.dot(params_ref[...], columns, preferred_element_type=F32)
    param_scale = lax.rsqrt(jnp.sum(params * params, axis=0, keepdims=True) + 1e-06)
    params = params.astype(BF16)
    copies[2].wait()
    copies[3].wait()
    gain = gain_ref[...].reshape(1, width)
    image_of = lax.broadcasted_iota(jnp.int32, (1, images * slots), 1) & 1
    dispatches = []
    block = 64
    for image in range(images):
        copies[1 if image == 0 else 4].wait()
        squares = []
        for at in range(0, tokens, block):
            floats = tokens_ref[image, at : at + block, :].astype(F32)
            centred = floats - jnp.mean(floats, axis=-1, keepdims=True)
            variance = jnp.mean(centred * centred, axis=-1, keepdims=True)
            normed = (centred * lax.rsqrt(variance + 1e-06) * gain).astype(BF16)
            normed_ref[image * tokens + at : image * tokens + at + block, :] = normed
            normed_f = normed.astype(F32)
            squares.append(jnp.sum(normed_f * normed_f, axis=-1, keepdims=True))
        token_scale = scale_ref[0] * lax.rsqrt(jnp.concatenate(squares, axis=0) + 1e-06)
        normed = normed_ref[image * tokens : (image + 1) * tokens, :]
        scores = jnp.dot(normed, params, preferred_element_type=F32)
        expo = jnp.exp(scores * token_scale * param_scale)
        expo = jnp.where(image_of == image, expo, 0.0)
        over_tokens = jnp.sum(expo, axis=0, keepdims=True)
        over_tokens = jnp.where(image_of == image, over_tokens, 1.0)
        dispatches.append((expo * (1.0 / over_tokens)).astype(BF16))
        combine_ref[image, :, :] = (expo * (1.0 / jnp.sum(expo, axis=1, keepdims=True))).astype(BF16)
        copies.append(pltpu.make_async_copy(combine_ref.at[image], combine_hbm.at[image], sems.at[5 + image]))
        copies[-1].start()
    dispatch = jnp.concatenate(dispatches, axis=0)
    places = slots_ref.shape[0] // 2
    for half in range(2):
        part = slice(half * places, (half + 1) * places)
        gathered = lax.dot_general(
            dispatch[:, half * slots : (half + 1) * slots],
            normed_ref[...],
            (((0,), (0,)), ((), ())),
            preferred_element_type=F32,
        ).astype(BF16)
        slots_ref[part] = gathered.reshape(places, *slots_ref.shape[1:])
        copies.append(pltpu.make_async_copy(slots_ref.at[part], slots_hbm.at[part], sems.at[7 + half]))
        copies[-1].start()
    for copy in copies[5:]:
        copy.wait()


def route(tokens, norm_gain, slot_params, logit_scale):
    images, count, width = tokens.shape
    slots = slot_params.shape[1]
    return pl.pallas_call(
        route_kernel,
        in_specs=[HBM] * 4,
        out_specs=[HBM] * 2,
        out_shape=[
            jax.ShapeDtypeStruct((slots // 2, 2, images, width), BF16),
            jax.ShapeDtypeStruct((images, count, images * slots), BF16),
        ],
        scratch_shapes=[
            pltpu.VMEM(tokens.shape, BF16),
            pltpu.VMEM(norm_gain.shape, F32),
            pltpu.VMEM(slot_params.shape, BF16),
            pltpu.SMEM(logit_scale.shape, F32),
            pltpu.VMEM((images * count, width), BF16),
            pltpu.VMEM((slots // 2, 2, images, width), BF16),
            pltpu.VMEM((images, count, images * slots), BF16),
            pltpu.SemaphoreType.DMA((9,)),
        ],
        compiler_params=limit(60),
        name="route",
    )(tokens, norm_gain, slot_params, logit_scale)


def expert_parts(rows, up_matrix, down_matrix):
    before = jnp.dot(rows, up_matrix, preferred_element_type=F32)
    hidden = (before * (0.5 + 0.5 * lax.erf(before * (0.5**0.5)))).astype(BF16)
    return jnp.dot(hidden, down_matrix, preferred_element_type=F32).astype(BF16)


def first_expert_kernel(rows_ref, up_hbm, down_hbm, out_ref, up_ref, down_ref, sems):
    up_copy = pltpu.make_async_copy(up_hbm.at[0], up_ref, sems.at[0])
    down_copy = pltpu.make_async_copy(down_hbm.at[0], down_ref, sems.at[1])
    up_copy.start()
    down_copy.start()
    up_copy.wait()
    down_copy.wait()
    up_ref[...] = up_ref[...].T
    part = expert_parts(rows_ref[...], up_ref[...], down_ref[...])
    out_ref[...] = part


def first_expert(group, up_matrix, down_matrix):
    return pl.pallas_call(
        first_expert_kernel,
        in_specs=[VMEM, HBM, HBM],
        out_specs=[VMEM] * 3,
        out_shape=[
            jax.ShapeDtypeStruct(group.shape, BF16),
            jax.ShapeDtypeStruct(up_matrix.shape[:0:-1], BF16),
            jax.ShapeDtypeStruct(down_matrix.shape[1:], BF16),
        ],
        scratch_shapes=[pltpu.SemaphoreType.DMA((2,))],
        compiler_params=limit(16),
        name="first_expert",
    )(group, up_matrix, down_matrix)


def expert_kernel(groups, *refs):
    up_ref, down_ref = refs[groups : groups + 2]
    outs = refs[groups + 2 :]
    flat = [ref[...] for ref in refs[:groups]]
    count = flat[0].shape[0]
    rows = flat[0] if groups == 1 else jnp.concatenate(flat, axis=0)
    part = expert_parts(rows, up_ref[...], down_ref[...])
    for at, out_ref in enumerate(outs):
        out_ref[...] = part[at * count : (at + 1) * count]


def expert(groups, up_matrix, down_matrix):
    return pl.pallas_call(
        lambda *refs: expert_kernel(len(groups), *refs),
        in_specs=[VMEM] * (len(groups) + 2),
        out_specs=[VMEM] * len(groups),
        out_shape=[jax.ShapeDtypeStruct(group.shape, BF16) for group in groups],
        compiler_params=limit(16),
        name="expert",
    )(*groups, up_matrix, down_matrix)


def split_kernel(arrived_ref, own_ref, other_ref):
    own_ref[...] = arrived_ref[:, 0, :, :].reshape(own_ref.shape)
    other_ref[...] = arrived_ref[:, 1, :, :].reshape(other_ref.shape)


def split(arrived):
    places, _, images, width = arrived.shape
    group = jax.ShapeDtypeStruct((places * images, width), BF16)
    return pl.pallas_call(
        split_kernel,
        in_specs=[VMEM],
        out_specs=[VMEM] * 2,
        out_shape=[group, group],
        compiler_params=limit(16),
        name="split",
    )(arrived)


def add_kernel(a_ref, b_ref, out_ref):
    out_ref[...] = (a_ref[...].astype(F32) + b_ref[...].astype(F32)).astype(BF16)


def add(a, b):
    return pl.pallas_call(
        add_kernel,
        in_specs=[VMEM] * 2,
        out_specs=VMEM,
        out_shape=jax.ShapeDtypeStruct(a.shape, BF16),
        compiler_params=limit(16),
        name="add",
    )(a, b)


def join_kernel(own_ref, a_ref, b_ref, out_ref):
    places, _, images, width = out_ref.shape
    out_ref[:, 0, :, :] = own_ref[...].reshape(places, images, width)
    total = (a_ref[...].astype(F32) + b_ref[...].astype(F32)).astype(BF16)
    out_ref[:, 1, :, :] = total.reshape(places, images, width)


def join(own, a, b):
    rows, width = own.shape
    return pl.pallas_call(
        join_kernel,
        in_specs=[VMEM] * 3,
        out_specs=VMEM,
        out_shape=jax.ShapeDtypeStruct((rows // IMAGES, 2, IMAGES, width), BF16),
        compiler_params=limit(16),
        name="join",
    )(own, a, b)


def mix_kernel(combine_ref, slots_ref, out_hbm, out_ref, sems):
    images, _, columns = combine_ref.shape
    slots = slots_ref[...].reshape(columns, -1)
    copies = []
    half = combine_ref.shape[1] // 2
    for image in range(images):
        for at in range(2):
            part = slice(at * half, (at + 1) * half)
            mixed = jnp.dot(combine_ref[image, part, :], slots, preferred_element_type=F32)
            out_ref[image, part, :] = mixed.astype(BF16)
            copies.append(
                pltpu.make_async_copy(out_ref.at[image, part], out_hbm.at[image, part], sems.at[image, at])
            )
            copies[-1].start()
    for copy in copies:
        copy.wait()


def mix(combine, slot_outputs):
    images, count, _ = combine.shape
    mixed = jax.ShapeDtypeStruct((images, count, slot_outputs.shape[-1]), BF16)
    return pl.pallas_call(
        mix_kernel,
        in_specs=[VMEM] * 2,
        out_specs=HBM,
        out_shape=mixed,
        scratch_shapes=[pltpu.VMEM(mixed.shape, BF16), pltpu.SemaphoreType.DMA((images, 2))],
        compiler_params=limit(16),
        name="mix",
    )(combine, slot_outputs)


def send(value, targets, back=False):
    pairs = [(2 * at + core, 2 * to + core) for core in range(2) for at, to in enumerate(targets[core])]
    return lax.ppermute(value, RING + ("core",), [pair[::-1] if back else pair for pair in pairs])


def exchange(value):
    return lax.all_to_all(value, PLANE, split_axis=0, concat_axis=0, tiled=True)


def local(tokens, norm_gain, slot_params, logit_scale, expert_up, expert_down):
    slot_inputs, combine = route(tokens, norm_gain, slot_params, logit_scale)
    own, other = split(exchange(slot_inputs))
    across, first, second = send(own, ACROSS), send(other, FIRST), send(other, SECOND)
    kept, up_matrix, down_matrix = first_expert(own, expert_up, expert_down)
    (across,) = expert([across], up_matrix, down_matrix)
    first, _ = lax.optimization_barrier((first, across))
    across = send(across, ACROSS, True)
    (first,) = expert([first], up_matrix, down_matrix)
    second, _ = lax.optimization_barrier((second, first))
    first = send(first, FIRST, True)
    (second,) = expert([second], up_matrix, down_matrix)
    second = send(second, SECOND, True)
    slot_outputs = join(add(kept, across), first, second)
    return mix(combine, exchange(slot_outputs))


def solution(mesh):
    fine = Mesh(mesh.devices.reshape(SIZES), AXES)
    expert_axes = AXES[1:]
    placed = (
        P(AXES, None, None),
        P(),
        P(),
        P(),
        P(expert_axes, "dp", None),
        P(expert_axes, "dp", None),
    )
    return jax.shard_map(
        local,
        mesh=fine,
        in_specs=placed,
        out_specs=P(AXES, None, None),
        check_vma=False,
    )
```

```python
import jax
import jax.numpy as jnp
from jax import lax
from jax.experimental import pallas as pl
from jax.experimental.pallas import tpu as pltpu
from jax.sharding import Mesh
from jax.sharding import PartitionSpec as P

BF16 = jnp.bfloat16
F32 = jnp.float32
MIB = 1024 * 1024
AXES = ("dp", "x", "y_lo", "z", "core")
SIZES = (2, 4, 2, 8, 2)
INNER = 16
PLANE = ("x", "z", "core")
RING = ("dp", "y_lo")
FIRST, SECOND, ACROSS = ((1, 2, 3, 0), (1, 2, 3, 0)), ((3, 0, 1, 2), (3, 0, 1, 2)), ((2, 3, 0, 1), (2, 3, 0, 1))
IMAGES = 2
VMEM = pl.BlockSpec(memory_space=pltpu.VMEM)
HBM = pl.BlockSpec(memory_space=pltpu.HBM)


def limit(mib):
    return pltpu.CompilerParams(vmem_limit_bytes=mib * MIB)


def column_slots(slots):
    column = lax.broadcasted_iota(jnp.int32, (1, IMAGES * slots), 1)
    slot = lax.broadcasted_iota(jnp.int32, (slots, IMAGES * slots), 0)
    group = (column >> 1) & 1
    place = column >> 2
    y_lo = (group + lax.axis_index("y_lo")) & 1
    wanted = (place >> 4) * (2 * INNER) + y_lo * INNER + (place & (INNER - 1))
    return (slot == wanted).astype(BF16)


def route_kernel(
    tokens_hbm, gain_hbm, params_hbm, scale_hbm, slots_hbm, combine_hbm,
    tokens_ref, gain_ref, params_ref, scale_ref, normed_ref, slots_ref, combine_ref, sems
):
    images, tokens, width = tokens_ref.shape
    copies = [
        pltpu.make_async_copy(params_hbm, params_ref, sems.at[0]),
        pltpu.make_async_copy(tokens_hbm.at[0], tokens_ref.at[0], sems.at[1]),
        pltpu.make_async_copy(gain_hbm, gain_ref, sems.at[2]),
        pltpu.make_async_copy(scale_hbm, scale_ref, sems.at[3]),
        pltpu.make_async_copy(tokens_hbm.at[1], tokens_ref.at[1], sems.at[4]),
    ]
    for copy in copies:
        copy.start()
    slots = params_ref.shape[1]
    columns = column_slots(slots)
    copies[0].wait()
    params = jnp.dot(params_ref[...], columns, preferred_element_type=F32)
    param_scale = lax.rsqrt(jnp.sum(params * params, axis=0, keepdims=True) + 1e-06)
    params = params.astype(BF16)
    copies[2].wait()
    copies[3].wait()
    gain = gain_ref[...].reshape(1, width)
    image_of = lax.broadcasted_iota(jnp.int32, (1, images * slots), 1) & 1
    dispatches = []
    block = 64
    for image in range(images):
        copies[1 if image == 0 else 4].wait()
        squares = []
        for at in range(0, tokens, block):
            floats = tokens_ref[image, at : at + block, :].astype(F32)
            centred = floats - jnp.mean(floats, axis=-1, keepdims=True)
            variance = jnp.mean(centred * centred, axis=-1, keepdims=True)
            normed = (centred * lax.rsqrt(variance + 1e-06) * gain).astype(BF16)
            normed_ref[image * tokens + at : image * tokens + at + block, :] = normed
            normed_f = normed.astype(F32)
            squares.append(jnp.sum(normed_f * normed_f, axis=-1, keepdims=True))
        token_scale = scale_ref[0] * lax.rsqrt(jnp.concatenate(squares, axis=0) + 1e-06)
        normed = normed_ref[image * tokens : (image + 1) * tokens, :]
        scores = jnp.dot(normed, params, preferred_element_type=F32)
        expo = jnp.exp(scores * token_scale * param_scale)
        expo = jnp.where(image_of == image, expo, 0.0)
        over_tokens = jnp.sum(expo, axis=0, keepdims=True)
        over_tokens = jnp.where(image_of == image, over_tokens, 1.0)
        dispatches.append((expo * (1.0 / over_tokens)).astype(BF16))
        combine_ref[image, :, :] = (expo * (1.0 / jnp.sum(expo, axis=1, keepdims=True))).astype(BF16)
        copies.append(pltpu.make_async_copy(combine_ref.at[image], combine_hbm.at[image], sems.at[5 + image]))
        copies[-1].start()
    dispatch = jnp.concatenate(dispatches, axis=0)
    places = slots_ref.shape[0] // 2
    for half in range(2):
        part = slice(half * places, (half + 1) * places)
        gathered = lax.dot_general(
            dispatch[:, half * slots : (half + 1) * slots],
            normed_ref[...],
            (((0,), (0,)), ((), ())),
            preferred_element_type=F32,
        ).astype(BF16)
        slots_ref[part] = gathered.reshape(places, *slots_ref.shape[1:])
        copies.append(pltpu.make_async_copy(slots_ref.at[part], slots_hbm.at[part], sems.at[7 + half]))
        copies[-1].start()
    for copy in copies[5:]:
        copy.wait()


def route(tokens, norm_gain, slot_params, logit_scale):
    images, count, width = tokens.shape
    slots = slot_params.shape[1]
    return pl.pallas_call(
        route_kernel,
        in_specs=[HBM] * 4,
        out_specs=[HBM] * 2,
        out_shape=[
            jax.ShapeDtypeStruct((slots // 2, 2, images, width), BF16),
            jax.ShapeDtypeStruct((images, count, images * slots), BF16),
        ],
        scratch_shapes=[
            pltpu.VMEM(tokens.shape, BF16),
            pltpu.VMEM(norm_gain.shape, F32),
            pltpu.VMEM(slot_params.shape, BF16),
            pltpu.SMEM(logit_scale.shape, F32),
            pltpu.VMEM((images * count, width), BF16),
            pltpu.VMEM((slots // 2, 2, images, width), BF16),
            pltpu.VMEM((images, count, images * slots), BF16),
            pltpu.SemaphoreType.DMA((9,)),
        ],
        compiler_params=limit(60),
        name="route",
    )(tokens, norm_gain, slot_params, logit_scale)


def expert_parts(rows, up_matrix, down_matrix):
    before = jnp.dot(rows, up_matrix, preferred_element_type=F32)
    hidden = (before * (0.5 + 0.5 * lax.erf(before * (0.5**0.5)))).astype(BF16)
    return jnp.dot(hidden, down_matrix, preferred_element_type=F32).astype(BF16)


def first_expert_kernel(rows_ref, up_hbm, down_hbm, out_ref, up_ref, down_ref, sems):
    up_copy = pltpu.make_async_copy(up_hbm.at[0], up_ref, sems.at[0])
    down_copy = pltpu.make_async_copy(down_hbm.at[0], down_ref, sems.at[1])
    up_copy.start()
    down_copy.start()
    up_copy.wait()
    down_copy.wait()
    up_ref[...] = up_ref[...].T
    part = expert_parts(rows_ref[...], up_ref[...], down_ref[...])
    out_ref[...] = part


def first_expert(group, up_matrix, down_matrix):
    return pl.pallas_call(
        first_expert_kernel,
        in_specs=[VMEM, HBM, HBM],
        out_specs=[VMEM] * 3,
        out_shape=[
            jax.ShapeDtypeStruct(group.shape, BF16),
            jax.ShapeDtypeStruct(up_matrix.shape[:0:-1], BF16),
            jax.ShapeDtypeStruct(down_matrix.shape[1:], BF16),
        ],
        scratch_shapes=[pltpu.SemaphoreType.DMA((2,))],
        compiler_params=limit(16),
        name="first_expert",
    )(group, up_matrix, down_matrix)


def expert_kernel(groups, *refs):
    up_ref, down_ref = refs[groups : groups + 2]
    outs = refs[groups + 2 :]
    flat = [ref[...] for ref in refs[:groups]]
    count = flat[0].shape[0]
    rows = flat[0] if groups == 1 else jnp.concatenate(flat, axis=0)
    part = expert_parts(rows, up_ref[...], down_ref[...])
    for at, out_ref in enumerate(outs):
        out_ref[...] = part[at * count : (at + 1) * count]


def expert(groups, up_matrix, down_matrix):
    return pl.pallas_call(
        lambda *refs: expert_kernel(len(groups), *refs),
        in_specs=[VMEM] * (len(groups) + 2),
        out_specs=[VMEM] * len(groups),
        out_shape=[jax.ShapeDtypeStruct(group.shape, BF16) for group in groups],
        compiler_params=limit(16),
        name="expert",
    )(*groups, up_matrix, down_matrix)


def split_kernel(arrived_ref, own_ref, other_ref):
    own_ref[...] = arrived_ref[:, 0, :, :].reshape(own_ref.shape)
    other_ref[...] = arrived_ref[:, 1, :, :].reshape(other_ref.shape)


def split(arrived):
    places, _, images, width = arrived.shape
    group = jax.ShapeDtypeStruct((places * images, width), BF16)
    return pl.pallas_call(
        split_kernel,
        in_specs=[VMEM],
        out_specs=[VMEM] * 2,
        out_shape=[group, group],
        compiler_params=limit(16),
        name="split",
    )(arrived)


def add_kernel(a_ref, b_ref, out_ref):
    out_ref[...] = (a_ref[...].astype(F32) + b_ref[...].astype(F32)).astype(BF16)


def add(a, b):
    return pl.pallas_call(
        add_kernel,
        in_specs=[VMEM] * 2,
        out_specs=VMEM,
        out_shape=jax.ShapeDtypeStruct(a.shape, BF16),
        compiler_params=limit(16),
        name="add",
    )(a, b)


def join_kernel(own_ref, a_ref, b_ref, out_ref):
    places, _, images, width = out_ref.shape
    out_ref[:, 0, :, :] = own_ref[...].reshape(places, images, width)
    total = (a_ref[...].astype(F32) + b_ref[...].astype(F32)).astype(BF16)
    out_ref[:, 1, :, :] = total.reshape(places, images, width)


def join(own, a, b):
    rows, width = own.shape
    return pl.pallas_call(
        join_kernel,
        in_specs=[VMEM] * 3,
        out_specs=VMEM,
        out_shape=jax.ShapeDtypeStruct((rows // IMAGES, 2, IMAGES, width), BF16),
        compiler_params=limit(16),
        name="join",
    )(own, a, b)


def mix_kernel(combine_ref, slots_ref, out_hbm, out_ref, sems):
    images, _, columns = combine_ref.shape
    slots = slots_ref[...].reshape(columns, -1)
    copies = []
    half = combine_ref.shape[1] // 2
    for image in range(images):
        for at in range(2):
            part = slice(at * half, (at + 1) * half)
            mixed = jnp.dot(combine_ref[image, part, :], slots, preferred_element_type=F32)
            out_ref[image, part, :] = mixed.astype(BF16)
            copies.append(
                pltpu.make_async_copy(out_ref.at[image, part], out_hbm.at[image, part], sems.at[image, at])
            )
            copies[-1].start()
    for copy in copies:
        copy.wait()


def mix(combine, slot_outputs):
    images, count, _ = combine.shape
    mixed = jax.ShapeDtypeStruct((images, count, slot_outputs.shape[-1]), BF16)
    return pl.pallas_call(
        mix_kernel,
        in_specs=[VMEM] * 2,
        out_specs=HBM,
        out_shape=mixed,
        scratch_shapes=[pltpu.VMEM(mixed.shape, BF16), pltpu.SemaphoreType.DMA((images, 2))],
        compiler_params=limit(16),
        name="mix",
    )(combine, slot_outputs)


def send(value, targets, back=False):
    pairs = [(2 * at + core, 2 * to + core) for core in range(2) for at, to in enumerate(targets[core])]
    return lax.ppermute(value, RING + ("core",), [pair[::-1] if back else pair for pair in pairs])


def exchange(value):
    return lax.all_to_all(value, PLANE, split_axis=0, concat_axis=0, tiled=True)


def local(tokens, norm_gain, slot_params, logit_scale, expert_up, expert_down):
    slot_inputs, combine = route(tokens, norm_gain, slot_params, logit_scale)
    own, other = split(exchange(slot_inputs))
    across, first, second = send(own, ACROSS), send(other, FIRST), send(other, SECOND)
    kept, up_matrix, down_matrix = first_expert(own, expert_up, expert_down)
    (across,) = expert([across], up_matrix, down_matrix)
    first, _ = lax.optimization_barrier((first, across))
    across = send(across, ACROSS, True)
    (first,) = expert([first], up_matrix, down_matrix)
    second, _ = lax.optimization_barrier((second, first))
    first = send(first, FIRST, True)
    (second,) = expert([second], up_matrix, down_matrix)
    second = send(second, SECOND, True)
    slot_outputs = join(add(kept, across), first, second)
    return mix(combine, exchange(slot_outputs))


def solution(mesh):
    fine = Mesh(mesh.devices.reshape(SIZES), AXES)
    expert_axes = AXES[1:]
    placed = (
        P(AXES, None, None),
        P(),
        P(),
        P(),
        P(expert_axes, "dp", None),
        P(expert_axes, "dp", None),
    )
    return jax.shard_map(
        local,
        mesh=fine,
        in_specs=placed,
        out_specs=P(AXES, None, None),
        check_vma=False,
    )
```
